32 devices in a mesh: tm: 8 (over z, core), row: 2 (over x), col: 2 (over y).
Axes of the slice: x: 2, y: 2, z: 4, core: 2. Of those that a mesh axis runs over, the one named last changes fastest.
Arguments:
- latents: bfloat16 [16, 64, 10240], P('tm', 'row', 'col'), may hold values from -6 to 6
- w_qkv: bfloat16 [320, 960], replicated, may hold values from -4 to 4
- w_out: bfloat16 [320, 320], replicated, may hold values from -0.3125 to 0.3125
- conv_weight: float32 [9, 320], replicated, may hold values from -1.8 to 1.8
Outputs:
- result: bfloat16 [16, 64, 10240], P('tm', 'row', 'col')
The draws below stay inside these ranges and needn't reach their ends.
All inputs are finite; a program needn't handle non-finite values.
Results may differ from the reference program's by a relative error of at most 0.013.
Values may be sent and summed in bfloat16 or wider, within the bound.
A program may use at most 64 MiB of HBM per device.

```python
import jax
import jax.numpy as jnp
from jax import lax

C = 320
HEAD_DIM = 64
FRAMES = 16
HEIGHT = 64
WIDTH = 32


def draw_w_qkv(key, part):
    base = jax.random.normal(key, (C, 3 * C), jnp.float32) * C ** (-0.5)
    return jnp.clip(base, -4.0, 4.0).astype(jnp.bfloat16)


def levels(own_key, shape, cuts, smallest, largest):
    gain, own = 1.0, jax.random.fold_in(own_key, 6)
    for axis_at, shards_of in cuts:
        steps = jnp.exp(jax.random.uniform(jax.random.fold_in(own, axis_at), (shards_of,), jnp.float32, smallest / len(cuts), largest / len(cuts)))
        gain = gain * jnp.repeat(steps, shape[axis_at] // shards_of).reshape([-1 if axis == axis_at else 1 for axis in range(len(shape))])
    return gain


def centred(stream_key, dims, deviation, bound, split=(), kind=jnp.bfloat16):
    drawn = jax.random.normal(stream_key, dims, jnp.float32) * deviation
    if len(split) > 0:
        drawn = levels(stream_key, dims, split, -0.22, 0.18) * drawn
    return jnp.clip(drawn, min=-bound, max=bound).astype(kind)


def setup_inputs(seed: int = 0) -> dict:
    streams_of = jax.random.split(jax.random.key(seed), 5)
    latents = centred(streams_of[0], (FRAMES, HEIGHT, WIDTH * C), 1.0, 6.0, ((0, 8), (1, 2), (2, 2)))
    w_qkv = draw_w_qkv(jax.random.fold_in(streams_of[4], 71), 0)
    w_out = centred(streams_of[2], (C, C), C ** -0.5, 0.3125)
    conv_weight = centred(streams_of[3], (9, C), 0.3, 1.8, (), jnp.float32)
    return dict(latents=latents, w_qkv=w_qkv, w_out=w_out, conv_weight=conv_weight)


def layer_norm(flat):
    mean = lax.optimization_barrier(jnp.mean(flat, axis=-1, keepdims=True))
    cent = flat - mean
    var = lax.optimization_barrier(jnp.mean(cent * cent, axis=-1, keepdims=True))
    return (cent * lax.rsqrt(var + 1e-05)).astype(jnp.bfloat16)

def window_attend(query, wide, first, total, heads, head_dim):
    frames = query.shape[0]
    points = query.shape[1]
    chans = heads * head_dim
    q_four = query.reshape(frames, points, heads, head_dim)
    scores = []
    values = []
    for shift_d in range(5):
        keys = wide[shift_d:shift_d + frames, :, :chans].reshape(frames, points, heads, head_dim)
        vals = wide[shift_d:shift_d + frames, :, chans:].reshape(frames, points, heads, head_dim)
        score = jnp.einsum('fphd,fphd->fph', q_four, keys, preferred_element_type=jnp.float32) * head_dim ** (-0.5)
        where_t = first + jnp.arange(frames, dtype=jnp.int32) + (shift_d - 2)
        valid = (where_t >= 0) & (where_t < total)
        scores.append(jnp.where(valid[:, None, None], score, jnp.float32(-1e+30)))
        values.append(vals)
    stacked = jnp.stack(scores, 0)
    top = lax.optimization_barrier(jnp.max(stacked, axis=0, keepdims=True))
    expo = jnp.exp(stacked - top)
    weights = (expo / lax.optimization_barrier(jnp.sum(expo, axis=0, keepdims=True))).astype(jnp.bfloat16)
    mixed = jnp.zeros((frames, points, heads, head_dim), jnp.float32)
    for shift_d in range(5):
        mixed = mixed + weights[shift_d].astype(jnp.float32)[..., None] * values[shift_d].astype(jnp.float32)
    return mixed.astype(jnp.bfloat16).reshape(frames * points, chans)

def reference(latents, w_qkv, w_out, conv_weight):
    frames, height, merged = latents.shape
    chans = w_out.shape[0]
    cols = merged // chans
    heads = chans // HEAD_DIM
    x_four = jnp.moveaxis(latents.reshape(frames, height, cols, chans), 1, 0)

    def strip(cells):
        flat = cells.reshape(frames * cols, chans).astype(jnp.float32)
        normed = layer_norm(flat)
        qkv = jnp.dot(normed, w_qkv, preferred_element_type=jnp.float32).astype(jnp.bfloat16)
        qkv = qkv.reshape(frames, cols, 3 * chans)
        pairs = qkv[:, :, chans:]
        zeros = jnp.zeros((2, cols, 2 * chans), jnp.bfloat16)
        wide = jnp.concatenate([zeros, pairs, zeros], 0)
        attended = window_attend(qkv[:, :, :chans], wide, jnp.int32(0), frames, heads, HEAD_DIM)
        proj = jnp.dot(attended, w_out, preferred_element_type=jnp.float32)
        return (flat + proj).astype(jnp.bfloat16).reshape(frames, cols, chans)
    hidden = jnp.moveaxis(lax.map(strip, x_four), 0, 1)

    def conv_frame(frame):
        padded = jnp.pad(frame, ((1, 1), (1, 1), (0, 0)))
        acc = frame.astype(jnp.float32)
        for tap_a in range(3):
            for tap_b in range(3):
                acc = acc + padded[tap_a:tap_a + height, tap_b:tap_b + cols, :].astype(jnp.float32) * conv_weight[3 * tap_a + tap_b]
        return acc.astype(jnp.bfloat16)
    result = lax.map(conv_frame, hidden)
    return result.reshape(frames, height, cols * chans)
```

```python
import functools

import jax
import jax.numpy as jnp
from jax import lax
from jax.experimental import pallas as pl
from jax.experimental.pallas import tpu as pltpu
from jax.sharding import PartitionSpec as P

HEAD_DIM = 64
LOG2E = 1.4426950408889634
MESH = pl.DeviceIdType.MESH
F32, BF16 = jnp.float32, jnp.bfloat16


def dot(a, b):
    return jnp.dot(a, b, preferred_element_type=F32)


def widen(even, odd, lane):
    mid = jnp.where(lane < 64, even, odd)
    return jnp.concatenate([even, even, mid, odd, odd], axis=1)


def kernel(
    sizes,
    x_ref, wqkv_ref, wout_ref, cw_ref, out_ref,
    norm, q_s, k_s, v_s, hid, swp, rowf, rows_out, rows_in, corn_in, edge,
    w1q, w2q, w3q, w1kv, w2kv, w3kv, w1o, w2o, w3o, taps, ones2, heads,
    t_send, t_recv, c_send, c_recv, r_send, r_recv, d_send, d_recv,
):
    n_t, n_r, n_c = sizes
    frames, rows, merged = x_ref.shape
    chans = wout_ref.shape[0]
    wide = 2 * chans
    pairs = merged // wide
    fr = frames * rows
    me_t, me_r, me_c = lax.axis_index("tm"), lax.axis_index("row"), lax.axis_index("col")

    has_t = (me_t > 0, me_t < n_t - 1)
    has_r = (me_r > 0, me_r < n_r - 1)
    has_c = (me_c > 0, me_c < n_c - 1)
    step = (-1, 1)
    near = []
    for s in range(2):
        near.append((has_t[s], (me_t + step[s], me_r, me_c)))
        near.append((has_r[s], (me_t, me_r + step[s], me_c)))
        near.append((has_c[s], (me_t, me_r, me_c + step[s])))
    diag = []
    for s in range(2):
        for u in range(2):
            diag.append(
                (has_r[s] & has_c[u], (me_t, me_r + step[s], me_c + step[u]), 2 * s + u)
            )
    barrier = pltpu.get_barrier_semaphore()
    count = jnp.int32(0)
    for ok, where in near + [d[:2] for d in diag]:
        @pl.when(ok)
        def _():
            pl.semaphore_signal(barrier, inc=1, device_id=where, device_id_type=MESH)
        count = count + jnp.where(ok, 1, 0).astype(jnp.int32)

    lane = lax.broadcasted_iota(jnp.int32, (1, 128), 1)

    at = lax.broadcasted_iota(jnp.int32, (wide, 256), 0)
    to = lax.broadcasted_iota(jnp.int32, (wide, 256), 1)
    ones2[...] = jnp.where((at < chans) == (to < 128), 1.0, 0.0).astype(BF16)
    at = lax.broadcasted_iota(jnp.int32, (256, 256), 0) // HEAD_DIM
    to = lax.broadcasted_iota(jnp.int32, (256, 256), 1) // HEAD_DIM
    heads[...] = jnp.where(at == to, 1.0, 0.0).astype(BF16)

    for s in range(2):
        @pl.when(jnp.logical_not(has_t[s]))
        def _():
            norm[:, s] = jnp.zeros((pairs, fr, wide), BF16)
        @pl.when(jnp.logical_not(has_c[s]))
        def _():
            swp[0 if s == 0 else pairs + 1] = jnp.zeros((fr, wide), BF16)
        @pl.when(jnp.logical_not(has_r[s]))
        def _():
            rows_in[s] = jnp.zeros(rows_in.shape[1:], BF16)
    for ok, _, i in diag:
        @pl.when(jnp.logical_not(ok))
        def _():
            corn_in[i] = jnp.zeros(corn_in.shape[1:], BF16)

    pl.semaphore_wait(barrier, count)

    def t_copy(s, p):
        return pltpu.make_async_remote_copy(
            src_ref=norm.at[p, 2], dst_ref=norm.at[p, 1 - s],
            send_sem=t_send.at[s, p], recv_sem=t_recv.at[1 - s, p],
            device_id=(me_t + step[s], me_r, me_c), device_id_type=MESH,
        )

    def normalise(p, carry):
        xb = x_ref[:, :, pl.ds(pl.multiple_of(p * wide, 128), wide)].reshape(fr, wide)
        sums = dot(xb, ones2[...]) * (1.0 / chans)
        cent = xb.astype(F32) - widen(sums[:, :128], sums[:, 128:], lane)
        var = dot((cent * cent).astype(BF16), ones2[...]) * (1.0 / chans)
        inv = lax.rsqrt(var + 1e-05)
        norm[p, 2] = (cent * widen(inv[:, :128], inv[:, 128:], lane)).astype(BF16)
        for s in range(2):
            @pl.when(has_t[s])
            def _():
                t_copy(s, p).start()
        return carry

    lax.fori_loop(0, pairs, normalise, 0)

    pad = wide - chans - 256
    def split(w32, r1, r2, r3, lo1, lo2):
        zero = jnp.zeros((chans, 64), F32)
        r1[0:chans, lo1:lo1 + 256] = w32[:, 0:256].astype(BF16)
        r1[chans:chans + pad, lo1:lo1 + 256] = jnp.zeros((pad, 256), BF16)
        r3[0:pad, lo1:lo1 + 256] = jnp.zeros((pad, 256), BF16)
        r3[pad:pad + chans, lo1:lo1 + 256] = w32[:, 64:320].astype(BF16)
        r2[0:chans, lo2:lo2 + 128] = jnp.concatenate([w32[:, 256:320], zero], 1).astype(BF16)
        r2[chans:, lo2:lo2 + 128] = jnp.concatenate([zero, w32[:, 0:64]], 1).astype(BF16)

    split(wqkv_ref[:, 0:chans].astype(F32), w1q, w2q, w3q, 0, 0)
    split(wqkv_ref[:, chans:2 * chans].astype(F32), w1kv, w2kv, w3kv, 0, 0)
    split(wqkv_ref[:, 2 * chans:].astype(F32), w1kv, w2kv, w3kv, 256, 128)
    split(wout_ref[...].astype(F32), w1o, w2o, w3o, 0, 0)
    taps[...] = jnp.concatenate([cw_ref[...], cw_ref[...]], 1)

    def project(a, r1, r2, r3):
        return jnp.concatenate(
            [dot(a[:, 0:384], r1[...]), dot(a, r2[...]), dot(a[:, 256:640], r3[...])], 1
        )

    def keys_values(a):
        o1 = dot(a[:, 0:384], w1kv[...]).astype(BF16)
        o2 = dot(a, w2kv[...]).astype(BF16)
        o3 = dot(a[:, 256:640], w3kv[...]).astype(BF16)
        keys = jnp.concatenate([o1[:, :256], o2[:, :128], o3[:, :256]], 1)
        vals = jnp.concatenate([o1[:, 256:], o2[:, 128:], o3[:, 256:]], 1)
        return keys, vals

    group = 2
    def own(g, carry):
        at = pl.ds(g * group, group)
        a = norm[at, 2].reshape(group * fr, wide)
        q = project(a, w1q, w2q, w3q) * (HEAD_DIM ** -0.5 * LOG2E)
        q_s[at] = q.astype(BF16).reshape(group, fr, wide)
        keys, vals = keys_values(a)
        k_s[at, 2] = keys.reshape(group, fr, wide)
        v_s[at, 2] = vals.reshape(group, fr, wide)
        return carry

    lax.fori_loop(0, pairs // group, own, 0)

    big = jnp.float32(3e38)
    caps = [jnp.where(has_t[s], big, jnp.float32(-1e30)) for s in range(2)]

    def place(w):
        slot = (0, 2, 1)[w // 2]
        return slot, (w % 2) * rows

    def attend(p, carry):
        for s in range(2):
            @pl.when(has_t[s])
            def _():
                t_copy(1 - s, p).wait_recv()
        keys, vals = keys_values(norm[p, 0:2].reshape(2 * fr, wide))
        k_s[p, 0:2] = keys.reshape(2, fr, wide)
        v_s[p, 0:2] = vals.reshape(2, fr, wide)
        outs = []
        for lo, hi in ((0, 256), (256, 512), (512, 640)):
            prods = []
            for f in range(2):
                q = q_s[p, f * rows:(f + 1) * rows, lo:hi]
                for d in range(5):
                    slot, r0 = place(f + d)
                    prods.append(q * k_s[p, slot, r0:r0 + rows, lo:hi])
            scores = dot(jnp.concatenate(prods, 0), heads[:hi - lo, :hi - lo])
            mixes = []
            for f in range(2):
                parts = []
                for d in range(5):
                    i = (f * 5 + d) * rows
                    part = scores[i:i + rows]
                    slot = place(f + d)[0]
                    if slot < 2:
                        part = jnp.minimum(part, caps[slot])
                    parts.append(part)
                top = functools.reduce(jnp.maximum, parts)
                total, mixed = None, None
                for d in range(5):
                    slot, r0 = place(f + d)
                    e = jnp.exp2(parts[d] - top)
                    m = e * v_s[p, slot, r0:r0 + rows, lo:hi].astype(F32)
                    total = e if d == 0 else total + e
                    mixed = m if d == 0 else mixed + m
                mixes.append((mixed / total).astype(BF16))
            outs.append(jnp.concatenate(mixes, 0))
        att = jnp.concatenate(outs, 1)
        xb = x_ref[:, :, pl.ds(pl.multiple_of(p * wide, 128), wide)].reshape(fr, wide)
        h = (xb.astype(F32) + project(att, w1o, w2o, w3o)).astype(BF16)
        hid[p] = h
        h32 = h.astype(F32)
        swp[p + 1] = pltpu.roll(h32, chans, 1).astype(BF16)
        for f in range(2):
            rowf[0, pl.ds(f * pairs + p, 1), :] = h32[f * rows:f * rows + 1]
            rowf[1, pl.ds(f * pairs + p, 1), :] = h32[(f + 1) * rows - 1:(f + 1) * rows]
        return carry

    lax.fori_loop(0, pairs, attend, 0)

    def c_copy(s):
        lanes = pl.ds(256, 384) if s == 0 else pl.ds(0, 384)
        return pltpu.make_async_remote_copy(
            src_ref=swp.at[1 if s == 0 else pairs, :, lanes],
            dst_ref=swp.at[pairs + 1 if s == 0 else 0, :, lanes],
            send_sem=c_send.at[s], recv_sem=c_recv.at[1 - s],
            device_id=(me_t, me_r, me_c + step[s]), device_id_type=MESH,
        )

    def r_copy(s):
        return pltpu.make_async_remote_copy(
            src_ref=rows_out.at[s], dst_ref=rows_in.at[1 - s],
            send_sem=r_send.at[s], recv_sem=r_recv.at[1 - s],
            device_id=(me_t, me_r + step[s], me_c), device_id_type=MESH,
        )

    def d_copy(i):
        return pltpu.make_async_remote_copy(
            src_ref=rows_out.at[i // 2], dst_ref=corn_in.at[3 - i],
            send_sem=d_send.at[i], recv_sem=d_recv.at[3 - i],
            device_id=diag[i][1], device_id_type=MESH,
        )

    rows_out[...] = rowf[...].astype(BF16)
    for s in range(2):
        @pl.when(has_r[s])
        def _():
            r_copy(s).start()
    for i in range(4):
        @pl.when(diag[i][0])
        def _():
            d_copy(i).start()
    for s in range(2):
        @pl.when(has_c[s])
        def _():
            c_copy(s).start()
    for s in range(2):
        @pl.when(has_c[s])
        def _():
            c_copy(1 - s).wait_recv()
        @pl.when(has_r[s])
        def _():
            r_copy(1 - s).wait_recv()
    for i in range(4):
        @pl.when(diag[i][0])
        def _():
            d_copy(3 - i).wait_recv()

    n_rows = rows_in.shape[1]
    pair_at = lax.broadcasted_iota(jnp.int32, (n_rows, 1), 0) % pairs
    first_half = lax.broadcasted_iota(jnp.int32, (1, wide), 1) < chans
    for s in range(2):
        line = rows_in[s].astype(F32)
        turned = pltpu.roll(line, chans, 1)
        left_c = pltpu.roll(corn_in[2 * s].astype(F32), chans, 1)
        right_c = pltpu.roll(corn_in[2 * s + 1].astype(F32), chans, 1)
        before = jnp.where(
            pair_at == 0, pltpu.roll(left_c, n_rows - (pairs - 1), 0), pltpu.roll(turned, 1, 0)
        )
        after = jnp.where(
            pair_at == pairs - 1,
            pltpu.roll(right_c, pairs - 1, 0),
            pltpu.roll(turned, n_rows - 1, 0),
        )
        tap = 6 * s
        edge[s] = (
            jnp.where(first_half, before, turned) * taps[tap:tap + 1]
            + line * taps[tap + 1:tap + 2]
            + jnp.where(first_half, turned, after) * taps[tap + 2:tap + 3]
        )

    row_at = lax.broadcasted_iota(jnp.int32, (rows, 1), 0)

    def convolve(p, carry):
        for f in range(2):
            at = pl.ds(f * rows, rows)
            h = hid[p, at].astype(F32)
            sw = swp[p + 1, at].astype(F32)
            mid_b = jnp.where(lane < 64, swp[p, at, 256:384].astype(F32), sw[:, 256:384])
            left = jnp.concatenate([swp[p, at, 0:256].astype(F32), mid_b, sw[:, 384:640]], 1)
            mid_a = jnp.where(lane < 64, sw[:, 256:384], swp[p + 2, at, 256:384].astype(F32))
            right = jnp.concatenate([sw[:, 0:256], mid_a, swp[p + 2, at, 384:640].astype(F32)], 1)
            acc = []
            for a in range(3):
                acc.append(
                    left * taps[3 * a:3 * a + 1]
                    + h * taps[3 * a + 1:3 * a + 2]
                    + right * taps[3 * a + 2:3 * a + 3]
                )
            above = edge[0, pl.ds(f * pairs + p, 1), :]
            below = edge[1, pl.ds(f * pairs + p, 1), :]
            down = jnp.where(row_at == 0, above, pltpu.roll(acc[0], 1, 0))
            up = jnp.where(row_at == rows - 1, below, pltpu.roll(acc[2], rows - 1, 0))
            res = (h + acc[1]) + (down + up)
            out_ref[f, :, pl.ds(pl.multiple_of(p * wide, 128), wide)] = res.astype(BF16)
        return carry

    lax.fori_loop(0, pairs, convolve, 0)

    for s in range(2):
        @pl.when(has_t[s])
        def _():
            def done(p, carry):
                t_copy(s, p).wait_send()
                return carry
            lax.fori_loop(0, pairs, done, 0)
        @pl.when(has_c[s])
        def _():
            c_copy(s).wait_send()
        @pl.when(has_r[s])
        def _():
            r_copy(s).wait_send()
    for i in range(4):
        @pl.when(diag[i][0])
        def _():
            d_copy(i).wait_send()


def body(sizes, latents, w_qkv, w_out, conv_weight):
    frames, rows, merged = latents.shape
    chans = w_out.shape[0]
    wide = 2 * chans
    pairs = merged // wide
    fr = frames * rows
    lines = -(-frames * pairs // 16) * 16
    vmem = pltpu.VMEM
    dma = pltpu.SemaphoreType.DMA
    scratch = [
        vmem((pairs, 3, fr, wide), BF16),
        vmem((pairs, fr, wide), BF16),
        vmem((pairs, 3, fr, wide), BF16),
        vmem((pairs, 3, fr, wide), BF16),
        vmem((pairs, fr, wide), BF16),
        vmem((pairs + 2, fr, wide), BF16),
        vmem((2, lines, wide), F32),
        vmem((2, lines, wide), BF16),
        vmem((2, lines, wide), BF16),
        vmem((4, lines, wide), BF16),
        vmem((2, lines, wide), F32),
        vmem((384, 256), BF16), vmem((wide, 128), BF16), vmem((384, 256), BF16),
        vmem((384, 512), BF16), vmem((wide, 256), BF16), vmem((384, 512), BF16),
        vmem((384, 256), BF16), vmem((wide, 128), BF16), vmem((384, 256), BF16),
        vmem((9, wide), F32),
        vmem((wide, 256), BF16),
        vmem((256, 256), BF16),
        dma((2, pairs)), dma((2, pairs)),
        dma((2,)), dma((2,)), dma((2,)), dma((2,)), dma((4,)), dma((4,)),
    ]
    cells = frames * rows * merged // chans
    return pl.pallas_call(
        functools.partial(kernel, sizes),
        out_shape=jax.ShapeDtypeStruct(latents.shape, BF16),
        in_specs=[pl.BlockSpec(memory_space=vmem)] * 4,
        out_specs=pl.BlockSpec(memory_space=vmem),
        scratch_shapes=scratch,
        compiler_params=pltpu.CompilerParams(
            collective_id=0, has_side_effects=True, vmem_limit_bytes=48 * 2**20
        ),
        cost_estimate=pl.CostEstimate(
            flops=2 * cells * chans * chans * 8, bytes_accessed=4 * cells * chans,
            transcendentals=cells * 25,
        ),
    )(latents, w_qkv, w_out, conv_weight)


def solution(mesh):
    sizes = tuple(mesh.shape[name] for name in ("tm", "row", "col"))
    placed = (P("tm", "row", "col"), P(), P(), P())
    return jax.shard_map(
        functools.partial(body, sizes), mesh=mesh, in_specs=placed,
        out_specs=P("tm", "row", "col"), check_vma=False,
    )
```

```python
import functools

import jax
import jax.numpy as jnp
from jax import lax
from jax.experimental import pallas as pl
from jax.experimental.pallas import tpu as pltpu
from jax.sharding import PartitionSpec as P

HEAD_DIM = 64
LOG2E = 1.4426950408889634
MESH = pl.DeviceIdType.MESH
F32, BF16 = jnp.float32, jnp.bfloat16


def dot(a, b):
    return jnp.dot(a, b, preferred_element_type=F32)


def widen(even, odd, lane):
    mid = jnp.where(lane < 64, even, odd)
    return jnp.concatenate([even, even, mid, odd, odd], axis=1)


def kernel(
    sizes,
    x_hbm, wqkv_hbm, wout_hbm, cw_hbm, out_ref,
    x_ref, wqkv_ref, wout_ref, cw_ref, acc_s,
    cells_in, q_s, k_s, v_s, hid, swp, rowf, rows_out, rows_in, corn_in, edge,
    w1q, w2q, w3q, w1kv, w2kv, w3kv, w1o, w2o, w3o, taps, ones2, heads,
    t_send, t_recv, c_send, c_recv, r_send, r_recv, d_send, d_recv, load,
):
    n_t, n_r, n_c = sizes
    loads = [
        pltpu.make_async_copy(src, dst, load.at[i])
        for i, (src, dst) in enumerate(
            ((x_hbm, x_ref), (wqkv_hbm, wqkv_ref), (wout_hbm, wout_ref), (cw_hbm, cw_ref))
        )
    ]
    for copy in loads:
        copy.start()
    frames, rows, merged = x_ref.shape
    chans = wout_ref.shape[0]
    wide = 2 * chans
    pairs = merged // wide
    fr = frames * rows
    me_t, me_r, me_c = lax.axis_index("tm"), lax.axis_index("row"), lax.axis_index("col")

    has_t = (me_t > 0, me_t < n_t - 1)
    has_r = (me_r > 0, me_r < n_r - 1)
    has_c = (me_c > 0, me_c < n_c - 1)
    step = (-1, 1)
    near = []
    for s in range(2):
        near.append((has_t[s], (me_t + step[s], me_r, me_c)))
        near.append((has_r[s], (me_t, me_r + step[s], me_c)))
        near.append((has_c[s], (me_t, me_r, me_c + step[s])))
    diag = []
    for s in range(2):
        for u in range(2):
            diag.append(
                (has_r[s] & has_c[u], (me_t, me_r + step[s], me_c + step[u]), 2 * s + u)
            )
    barrier = pltpu.get_barrier_semaphore()
    count = jnp.int32(0)
    for ok, where in near + [d[:2] for d in diag]:
        @pl.when(ok)
        def _():
            pl.semaphore_signal(barrier, inc=1, device_id=where, device_id_type=MESH)
        count = count + jnp.where(ok, 1, 0).astype(jnp.int32)

    pl.semaphore_wait(barrier, count)

    def t_copy(s, p):
        return pltpu.make_async_remote_copy(
            src_ref=x_hbm.at[:, :, pl.ds(pl.multiple_of(p * wide, 128), wide)],
            dst_ref=cells_in.at[p, 1 - s],
            send_sem=t_send.at[s, p], recv_sem=t_recv.at[1 - s, p],
            device_id=(me_t + step[s], me_r, me_c), device_id_type=MESH,
        )

    def turn(k):
        return jnp.where(k == 0, 0, jnp.where(k == 1, pairs - 1, k - 1))

    def send(k, carry):
        for s in range(2):
            @pl.when(has_t[s])
            def _():
                t_copy(s, turn(k)).start()
        return carry

    lax.fori_loop(0, pairs, send, 0)

    lane = lax.broadcasted_iota(jnp.int32, (1, 128), 1)

    at = lax.broadcasted_iota(jnp.int32, (wide, 256), 0)
    to = lax.broadcasted_iota(jnp.int32, (wide, 256), 1)
    ones2[...] = jnp.where((at < chans) == (to < 128), 1.0, 0.0).astype(BF16)
    at = lax.broadcasted_iota(jnp.int32, (256, 256), 0) // HEAD_DIM
    to = lax.broadcasted_iota(jnp.int32, (256, 256), 1) // HEAD_DIM
    heads[...] = jnp.where(at == to, 1.0, 0.0).astype(BF16)

    for s in range(2):
        @pl.when(jnp.logical_not(has_t[s]))
        def _():
            cells_in[:, s] = jnp.zeros((pairs, frames, rows, wide), BF16)
        @pl.when(jnp.logical_not(has_c[s]))
        def _():
            swp[0 if s == 0 else pairs + 1] = jnp.zeros((fr, wide), BF16)
        @pl.when(jnp.logical_not(has_r[s]))
        def _():
            rows_in[s] = jnp.zeros(rows_in.shape[1:], BF16)
    for ok, _, i in diag:
        @pl.when(jnp.logical_not(ok))
        def _():
            corn_in[i] = jnp.zeros(corn_in.shape[1:], BF16)

    def normalise(xb):
        sums = dot(xb, ones2[...]) * (1.0 / chans)
        cent = xb.astype(F32) - widen(sums[:, :128], sums[:, 128:], lane)
        var = dot((cent * cent).astype(BF16), ones2[...]) * (1.0 / chans)
        inv = lax.rsqrt(var + 1e-05)
        return (cent * widen(inv[:, :128], inv[:, 128:], lane)).astype(BF16)

    def mine(p):
        return x_ref[:, :, pl.ds(pl.multiple_of(p * wide, 128), wide)].reshape(fr, wide)

    for copy in loads[1:]:
        copy.wait()

    pad = wide - chans - 256
    def split(w32, r1, r2, r3, lo1, lo2):
        zero = jnp.zeros((chans, 64), F32)
        r1[0:chans, lo1:lo1 + 256] = w32[:, 0:256].astype(BF16)
        r1[chans:chans + pad, lo1:lo1 + 256] = jnp.zeros((pad, 256), BF16)
        r3[0:pad, lo1:lo1 + 256] = jnp.zeros((pad, 256), BF16)
        r3[pad:pad + chans, lo1:lo1 + 256] = w32[:, 64:320].astype(BF16)
        r2[0:chans, lo2:lo2 + 128] = jnp.concatenate([w32[:, 256:320], zero], 1).astype(BF16)
        r2[chans:, lo2:lo2 + 128] = jnp.concatenate([zero, w32[:, 0:64]], 1).astype(BF16)

    split(wqkv_ref[:, 0:chans].astype(F32), w1q, w2q, w3q, 0, 0)
    split(wqkv_ref[:, chans:2 * chans].astype(F32), w1kv, w2kv, w3kv, 0, 0)
    split(wqkv_ref[:, 2 * chans:].astype(F32), w1kv, w2kv, w3kv, 256, 128)
    split(wout_ref[...].astype(F32), w1o, w2o, w3o, 0, 0)
    taps[...] = jnp.concatenate([cw_ref[...], cw_ref[...]], 1)

    def project(a, r1, r2, r3):
        return jnp.concatenate(
            [dot(a[:, 0:384], r1[...]), dot(a, r2[...]), dot(a[:, 256:640], r3[...])], 1
        )

    def keys_values(a):
        o1 = dot(a[:, 0:384], w1kv[...]).astype(BF16)
        o2 = dot(a, w2kv[...]).astype(BF16)
        o3 = dot(a[:, 256:640], w3kv[...]).astype(BF16)
        keys = jnp.concatenate([o1[:, :256], o2[:, :128], o3[:, :256]], 1)
        vals = jnp.concatenate([o1[:, 256:], o2[:, 128:], o3[:, 256:]], 1)
        return keys, vals

    loads[0].wait()
    group = 2
    def own(g, carry):
        at = pl.ds(g * group, group)
        a = jnp.concatenate([normalise(mine(g * group + i)) for i in range(group)], 0)
        q = project(a, w1q, w2q, w3q) * (HEAD_DIM ** -0.5 * LOG2E)
        q_s[at] = q.astype(BF16).reshape(group, fr, wide)
        keys, vals = keys_values(a)
        k_s[at, 2] = keys.reshape(group, fr, wide)
        v_s[at, 2] = vals.reshape(group, fr, wide)
        return carry

    lax.fori_loop(0, pairs // group, own, 0)

    big = jnp.float32(3e38)
    caps = [jnp.where(has_t[s], big, jnp.float32(-1e30)) for s in range(2)]

    def place(w):
        slot = (0, 2, 1)[w // 2]
        return slot, (w % 2) * rows

    def c_copy(s):
        lanes = pl.ds(256, 384) if s == 0 else pl.ds(0, 384)
        return pltpu.make_async_remote_copy(
            src_ref=swp.at[1 if s == 0 else pairs, :, lanes],
            dst_ref=swp.at[pairs + 1 if s == 0 else 0, :, lanes],
            send_sem=c_send.at[s], recv_sem=c_recv.at[1 - s],
            device_id=(me_t, me_r, me_c + step[s]), device_id_type=MESH,
        )

    def attend(k, carry):
        p = turn(k)
        for s in range(2):
            @pl.when(has_t[s])
            def _():
                t_copy(1 - s, p).wait_recv()
        keys, vals = keys_values(normalise(cells_in[p].reshape(2 * fr, wide)))
        k_s[p, 0:2] = keys.reshape(2, fr, wide)
        v_s[p, 0:2] = vals.reshape(2, fr, wide)
        outs = []
        for lo, hi in ((0, 256), (256, 512), (512, 640)):
            prods = []
            for f in range(2):
                q = q_s[p, f * rows:(f + 1) * rows, lo:hi]
                for d in range(5):
                    slot, r0 = place(f + d)
                    prods.append(q * k_s[p, slot, r0:r0 + rows, lo:hi])
            scores = dot(jnp.concatenate(prods, 0), heads[:hi - lo, :hi - lo])
            mixes = []
            for f in range(2):
                parts = []
                for d in range(5):
                    i = (f * 5 + d) * rows
                    part = scores[i:i + rows]
                    slot = place(f + d)[0]
                    if slot < 2:
                        part = jnp.minimum(part, caps[slot])
                    parts.append(part)
                top = functools.reduce(jnp.maximum, parts)
                total, mixed = None, None
                for d in range(5):
                    slot, r0 = place(f + d)
                    e = jnp.exp2(parts[d] - top)
                    m = e * v_s[p, slot, r0:r0 + rows, lo:hi].astype(F32)
                    total = e if d == 0 else total + e
                    mixed = m if d == 0 else mixed + m
                mixes.append((mixed / total).astype(BF16))
            outs.append(jnp.concatenate(mixes, 0))
        att = jnp.concatenate(outs, 1)
        h = (mine(p).astype(F32) + project(att, w1o, w2o, w3o)).astype(BF16)
        hid[p] = h
        h32 = h.astype(F32)
        swp[p + 1] = pltpu.roll(h32, chans, 1).astype(BF16)
        for f in range(2):
            rowf[0, pl.ds(f * pairs + p, 1), :] = h32[f * rows:f * rows + 1]
            rowf[1, pl.ds(f * pairs + p, 1), :] = h32[(f + 1) * rows - 1:(f + 1) * rows]
        for s in range(2):
            @pl.when(has_c[s] & (k == s))
            def _():
                c_copy(s).start()
        return carry

    lax.fori_loop(0, pairs, attend, 0)

    def r_copy(s):
        return pltpu.make_async_remote_copy(
            src_ref=rows_out.at[s], dst_ref=rows_in.at[1 - s],
            send_sem=r_send.at[s], recv_sem=r_recv.at[1 - s],
            device_id=(me_t, me_r + step[s], me_c), device_id_type=MESH,
        )

    def d_copy(i):
        return pltpu.make_async_remote_copy(
            src_ref=rows_out.at[i // 2], dst_ref=corn_in.at[3 - i],
            send_sem=d_send.at[i], recv_sem=d_recv.at[3 - i],
            device_id=diag[i][1], device_id_type=MESH,
        )

    rows_out[...] = rowf[...].astype(BF16)
    for s in range(2):
        @pl.when(has_r[s])
        def _():
            r_copy(s).start()
    for i in range(4):
        @pl.when(diag[i][0])
        def _():
            d_copy(i).start()
    for s in range(2):
        @pl.when(has_c[s])
        def _():
            c_copy(1 - s).wait_recv()

    row_at = lax.broadcasted_iota(jnp.int32, (rows, 1), 0)

    def convolve(p, carry):
        for f in range(2):
            at = pl.ds(f * rows, rows)
            h = hid[p, at].astype(F32)
            sw = swp[p + 1, at].astype(F32)
            mid_b = jnp.where(lane < 64, swp[p, at, 256:384].astype(F32), sw[:, 256:384])
            left = jnp.concatenate([swp[p, at, 0:256].astype(F32), mid_b, sw[:, 384:640]], 1)
            mid_a = jnp.where(lane < 64, sw[:, 256:384], swp[p + 2, at, 256:384].astype(F32))
            right = jnp.concatenate([sw[:, 0:256], mid_a, swp[p + 2, at, 384:640].astype(F32)], 1)
            acc = []
            for a in range(3):
                acc.append(
                    left * taps[3 * a:3 * a + 1]
                    + h * taps[3 * a + 1:3 * a + 2]
                    + right * taps[3 * a + 2:3 * a + 3]
                )
            down = jnp.where(row_at == 0, 0.0, pltpu.roll(acc[0], 1, 0))
            up = jnp.where(row_at == rows - 1, 0.0, pltpu.roll(acc[2], rows - 1, 0))
            acc_s[p, f] = (h + acc[1]) + (down + up)
        return carry

    lax.fori_loop(0, pairs, convolve, 0)

    for s in range(2):
        @pl.when(has_r[s])
        def _():
            r_copy(1 - s).wait_recv()
    for i in range(4):
        @pl.when(diag[i][0])
        def _():
            d_copy(3 - i).wait_recv()

    n_rows = rows_in.shape[1]
    pair_at = lax.broadcasted_iota(jnp.int32, (n_rows, 1), 0) % pairs
    first_half = lax.broadcasted_iota(jnp.int32, (1, wide), 1) < chans
    for s in range(2):
        line = rows_in[s].astype(F32)
        turned = pltpu.roll(line, chans, 1)
        left_c = pltpu.roll(corn_in[2 * s].astype(F32), chans, 1)
        right_c = pltpu.roll(corn_in[2 * s + 1].astype(F32), chans, 1)
        before = jnp.where(
            pair_at == 0, pltpu.roll(left_c, n_rows - (pairs - 1), 0), pltpu.roll(turned, 1, 0)
        )
        after = jnp.where(
            pair_at == pairs - 1,
            pltpu.roll(right_c, pairs - 1, 0),
            pltpu.roll(turned, n_rows - 1, 0),
        )
        tap = 6 * s
        edge[s] = (
            jnp.where(first_half, before, turned) * taps[tap:tap + 1]
            + line * taps[tap + 1:tap + 2]
            + jnp.where(first_half, turned, after) * taps[tap + 2:tap + 3]
        )

    def finish(p, carry):
        for f in range(2):
            above = edge[0, pl.ds(f * pairs + p, 1), :]
            below = edge[1, pl.ds(f * pairs + p, 1), :]
            head = acc_s[p, f, 0:8] + jnp.where(row_at[0:8] == 0, above, 0.0)
            foot = acc_s[p, f, rows - 8:] + jnp.where(row_at[rows - 8:] == rows - 1, below, 0.0)
            res = jnp.concatenate([head, acc_s[p, f, 8:rows - 8], foot], 0)
            out_ref[f, :, pl.ds(pl.multiple_of(p * wide, 128), wide)] = res.astype(BF16)
        return carry

    lax.fori_loop(0, pairs, finish, 0)

    for s in range(2):
        @pl.when(has_t[s])
        def _():
            def done(p, carry):
                t_copy(s, p).wait_send()
                return carry
            lax.fori_loop(0, pairs, done, 0)
        @pl.when(has_c[s])
        def _():
            c_copy(s).wait_send()
        @pl.when(has_r[s])
        def _():
            r_copy(s).wait_send()
    for i in range(4):
        @pl.when(diag[i][0])
        def _():
            d_copy(i).wait_send()


def body(sizes, latents, w_qkv, w_out, conv_weight):
    frames, rows, merged = latents.shape
    chans = w_out.shape[0]
    wide = 2 * chans
    pairs = merged // wide
    fr = frames * rows
    lines = -(-frames * pairs // 16) * 16
    vmem = pltpu.VMEM
    dma = pltpu.SemaphoreType.DMA
    scratch = [
        vmem(latents.shape, BF16), vmem(w_qkv.shape, BF16),
        vmem(w_out.shape, BF16), vmem(conv_weight.shape, F32),
        vmem((pairs, frames, rows, wide), F32),
        vmem((pairs, 2, frames, rows, wide), BF16),
        vmem((pairs, fr, wide), BF16),
        vmem((pairs, 3, fr, wide), BF16),
        vmem((pairs, 3, fr, wide), BF16),
        vmem((pairs, fr, wide), BF16),
        vmem((pairs + 2, fr, wide), BF16),
        vmem((2, lines, wide), F32),
        vmem((2, lines, wide), BF16),
        vmem((2, lines, wide), BF16),
        vmem((4, lines, wide), BF16),
        vmem((2, lines, wide), F32),
        vmem((384, 256), BF16), vmem((wide, 128), BF16), vmem((384, 256), BF16),
        vmem((384, 512), BF16), vmem((wide, 256), BF16), vmem((384, 512), BF16),
        vmem((384, 256), BF16), vmem((wide, 128), BF16), vmem((384, 256), BF16),
        vmem((9, wide), F32),
        vmem((wide, 256), BF16),
        vmem((256, 256), BF16),
        dma((2, pairs)), dma((2, pairs)),
        dma((2,)), dma((2,)), dma((2,)), dma((2,)), dma((4,)), dma((4,)), dma((4,)),
    ]
    cells = frames * rows * merged // chans
    return pl.pallas_call(
        functools.partial(kernel, sizes),
        out_shape=jax.ShapeDtypeStruct(latents.shape, BF16),
        in_specs=[pl.BlockSpec(memory_space=pl.ANY)] * 4,
        out_specs=pl.BlockSpec(memory_space=vmem),
        scratch_shapes=scratch,
        compiler_params=pltpu.CompilerParams(
            collective_id=0, has_side_effects=True, vmem_limit_bytes=56 * 2**20
        ),
        cost_estimate=pl.CostEstimate(
            flops=2 * cells * chans * chans * 8, bytes_accessed=4 * cells * chans,
            transcendentals=cells * 25,
        ),
    )(latents, w_qkv, w_out, conv_weight)


def solution(mesh):
    sizes = tuple(mesh.shape[name] for name in ("tm", "row", "col"))
    placed = (P("tm", "row", "col"), P(), P(), P())
    return jax.shard_map(
        functools.partial(body, sizes), mesh=mesh, in_specs=placed,
        out_specs=P("tm", "row", "col"), check_vma=False,
    )
```

```python
import functools

import jax
import jax.numpy as jnp
from jax import lax
from jax.experimental import pallas as pl
from jax.experimental.pallas import tpu as pltpu
from jax.sharding import PartitionSpec as P

HEAD_DIM = 64
LOG2E = 1.4426950408889634
MESH = pl.DeviceIdType.MESH
F32, BF16 = jnp.float32, jnp.bfloat16


def dot(a, b):
    return jnp.dot(a, b, preferred_element_type=F32)


def widen(even, odd, lane):
    mid = jnp.where(lane < 64, even, odd)
    return jnp.concatenate([even, even, mid, odd, odd], axis=1)


def kernel(
    sizes,
    x_hbm, wqkv_hbm, wout_hbm, cw_hbm, out_ref,
    x_ref, wqkv_ref, wout_ref, cw_ref, acc_s,
    cells_in, q_s, k_s, v_s, hid, swp, rowf, rows_out, rows_in, corn_in, edge,
    w1q, w2q, w3q, w1kv, w2kv, w3kv, w1o, w2o, w3o, taps, ones2, heads,
    t_send, t_recv, c_send, c_recv, r_send, r_recv, d_send, d_recv, load,
):
    n_t, n_r, n_c = sizes
    loads = [
        pltpu.make_async_copy(src, dst, load.at[i])
        for i, (src, dst) in enumerate(
            ((x_hbm, x_ref), (wqkv_hbm, wqkv_ref), (wout_hbm, wout_ref), (cw_hbm, cw_ref))
        )
    ]
    for copy in loads:
        copy.start()
    frames, rows, merged = x_ref.shape
    chans = wout_ref.shape[0]
    wide = 2 * chans
    pairs = merged // wide
    fr = frames * rows
    me_t, me_r, me_c = lax.axis_index("tm"), lax.axis_index("row"), lax.axis_index("col")

    has_t = (me_t > 0, me_t < n_t - 1)
    has_r = (me_r > 0, me_r < n_r - 1)
    has_c = (me_c > 0, me_c < n_c - 1)
    step = (-1, 1)
    near = []
    for s in range(2):
        near.append((has_t[s], (me_t + step[s], me_r, me_c)))
        near.append((has_r[s], (me_t, me_r + step[s], me_c)))
        near.append((has_c[s], (me_t, me_r, me_c + step[s])))
    diag = []
    for s in range(2):
        for u in range(2):
            diag.append(
                (has_r[s] & has_c[u], (me_t, me_r + step[s], me_c + step[u]), 2 * s + u)
            )
    barrier = pltpu.get_barrier_semaphore()
    count = jnp.int32(0)
    for ok, where in near + [d[:2] for d in diag]:
        @pl.when(ok)
        def _():
            pl.semaphore_signal(barrier, inc=1, device_id=where, device_id_type=MESH)
        count = count + jnp.where(ok, 1, 0).astype(jnp.int32)

    pl.semaphore_wait(barrier, count)

    def t_copy(s, p):
        return pltpu.make_async_remote_copy(
            src_ref=x_hbm.at[:, :, pl.ds(pl.multiple_of(p * wide, 128), wide)],
            dst_ref=cells_in.at[p, 1 - s],
            send_sem=t_send.at[s, p], recv_sem=t_recv.at[1 - s, p],
            device_id=(me_t + step[s], me_r, me_c), device_id_type=MESH,
        )

    def turn(k):
        return jnp.where(k == 0, 0, jnp.where(k == 1, pairs - 1, k - 1))

    def send(k, carry):
        for s in range(2):
            @pl.when(has_t[s])
            def _():
                t_copy(s, turn(k)).start()
        return carry

    lax.fori_loop(0, pairs, send, 0)

    lane = lax.broadcasted_iota(jnp.int32, (1, 128), 1)

    at = lax.broadcasted_iota(jnp.int32, (wide, 256), 0)
    to = lax.broadcasted_iota(jnp.int32, (wide, 256), 1)
    ones2[...] = jnp.where((at < chans) == (to < 128), 1.0, 0.0).astype(BF16)
    at = lax.broadcasted_iota(jnp.int32, (256, 256), 0) // HEAD_DIM
    to = lax.broadcasted_iota(jnp.int32, (256, 256), 1) // HEAD_DIM
    heads[...] = jnp.where(at == to, 1.0, 0.0).astype(BF16)

    for s in range(2):
        @pl.when(jnp.logical_not(has_t[s]))
        def _():
            cells_in[:, s] = jnp.zeros((pairs, frames, rows, wide), BF16)
        @pl.when(jnp.logical_not(has_c[s]))
        def _():
            swp[0 if s == 0 else pairs + 1] = jnp.zeros((fr, wide), BF16)
        @pl.when(jnp.logical_not(has_r[s]))
        def _():
            rows_in[s] = jnp.zeros(rows_in.shape[1:], BF16)
    for ok, _, i in diag:
        @pl.when(jnp.logical_not(ok))
        def _():
            corn_in[i] = jnp.zeros(corn_in.shape[1:], BF16)

    def normalise(xb):
        sums = dot(xb, ones2[...]) * (1.0 / chans)
        cent = xb.astype(F32) - widen(sums[:, :128], sums[:, 128:], lane)
        var = dot((cent * cent).astype(BF16), ones2[...]) * (1.0 / chans)
        inv = lax.rsqrt(var + 1e-05)
        return (cent * widen(inv[:, :128], inv[:, 128:], lane)).astype(BF16)

    def mine(p):
        return x_ref[:, :, pl.ds(pl.multiple_of(p * wide, 128), wide)].reshape(fr, wide)

    for copy in loads[1:]:
        copy.wait()

    pad = wide - chans - 256
    def split(w32, r1, r2, r3, lo1, lo2):
        zero = jnp.zeros((chans, 64), F32)
        r1[0:chans, lo1:lo1 + 256] = w32[:, 0:256].astype(BF16)
        r1[chans:chans + pad, lo1:lo1 + 256] = jnp.zeros((pad, 256), BF16)
        r3[0:pad, lo1:lo1 + 256] = jnp.zeros((pad, 256), BF16)
        r3[pad:pad + chans, lo1:lo1 + 256] = w32[:, 64:320].astype(BF16)
        r2[0:chans, lo2:lo2 + 128] = jnp.concatenate([w32[:, 256:320], zero], 1).astype(BF16)
        r2[chans:, lo2:lo2 + 128] = jnp.concatenate([zero, w32[:, 0:64]], 1).astype(BF16)

    split(wqkv_ref[:, 0:chans].astype(F32), w1q, w2q, w3q, 0, 0)
    split(wqkv_ref[:, chans:2 * chans].astype(F32), w1kv, w2kv, w3kv, 0, 0)
    split(wqkv_ref[:, 2 * chans:].astype(F32), w1kv, w2kv, w3kv, 256, 128)
    split(wout_ref[...].astype(F32), w1o, w2o, w3o, 0, 0)
    taps[...] = jnp.concatenate([cw_ref[...], cw_ref[...]], 1)

    def project(a, r1, r2, r3):
        return jnp.concatenate(
            [dot(a[:, 0:384], r1[...]), dot(a, r2[...]), dot(a[:, 256:640], r3[...])], 1
        )

    def keys_values(a):
        o1 = dot(a[:, 0:384], w1kv[...]).astype(BF16)
        o2 = dot(a, w2kv[...]).astype(BF16)
        o3 = dot(a[:, 256:640], w3kv[...]).astype(BF16)
        keys = jnp.concatenate([o1[:, :256], o2[:, :128], o3[:, :256]], 1)
        vals = jnp.concatenate([o1[:, 256:], o2[:, 128:], o3[:, 256:]], 1)
        return keys, vals

    loads[0].wait()
    group = 2
    def own(g, carry):
        at = pl.ds(g * group, group)
        a = jnp.concatenate([normalise(mine(g * group + i)) for i in range(group)], 0)
        q = project(a, w1q, w2q, w3q) * (HEAD_DIM ** -0.5 * LOG2E)
        q_s[at] = q.astype(BF16).reshape(group, fr, wide)
        keys, vals = keys_values(a)
        k_s[at, 2] = keys.reshape(group, fr, wide)
        v_s[at, 2] = vals.reshape(group, fr, wide)
        return carry

    lax.fori_loop(0, pairs // group, own, 0)

    big = jnp.float32(3e38)
    caps = [jnp.where(has_t[s], big, jnp.float32(-1e30)) for s in range(2)]

    def place(w):
        slot = (0, 2, 1)[w // 2]
        return slot, (w % 2) * rows

    def c_copy(s):
        lanes = pl.ds(256, 384) if s == 0 else pl.ds(0, 384)
        return pltpu.make_async_remote_copy(
            src_ref=swp.at[1 if s == 0 else pairs, :, lanes],
            dst_ref=swp.at[pairs + 1 if s == 0 else 0, :, lanes],
            send_sem=c_send.at[s], recv_sem=c_recv.at[1 - s],
            device_id=(me_t, me_r, me_c + step[s]), device_id_type=MESH,
        )

    def attend(k, carry):
        p = turn(k)
        for s in range(2):
            @pl.when(has_t[s])
            def _():
                t_copy(1 - s, p).wait_recv()
        keys, vals = keys_values(normalise(cells_in[p].reshape(2 * fr, wide)))
        k_s[p, 0:2] = keys.reshape(2, fr, wide)
        v_s[p, 0:2] = vals.reshape(2, fr, wide)
        outs = []
        for lo, hi in ((0, 256), (256, 512), (512, 640)):
            prods = []
            for f in range(2):
                q = q_s[p, f * rows:(f + 1) * rows, lo:hi]
                for d in range(5):
                    slot, r0 = place(f + d)
                    prods.append(q * k_s[p, slot, r0:r0 + rows, lo:hi])
            scores = dot(jnp.concatenate(prods, 0), heads[:hi - lo, :hi - lo])
            mixes = []
            for f in range(2):
                parts = []
                for d in range(5):
                    i = (f * 5 + d) * rows
                    part = scores[i:i + rows]
                    slot = place(f + d)[0]
                    if slot < 2:
                        part = jnp.minimum(part, caps[slot])
                    parts.append(part)
                top = functools.reduce(jnp.maximum, parts)
                total, mixed = None, None
                for d in range(5):
                    slot, r0 = place(f + d)
                    e = jnp.exp2(parts[d] - top)
                    m = e * v_s[p, slot, r0:r0 + rows, lo:hi].astype(F32)
                    total = e if d == 0 else total + e
                    mixed = m if d == 0 else mixed + m
                mixes.append((mixed / total).astype(BF16))
            outs.append(jnp.concatenate(mixes, 0))
        att = jnp.concatenate(outs, 1)
        h = (mine(p).astype(F32) + project(att, w1o, w2o, w3o)).astype(BF16)
        hid[p] = h
        h32 = h.astype(F32)
        swp[p + 1] = pltpu.roll(h32, chans, 1).astype(BF16)
        for f in range(2):
            rowf[0, pl.ds(f * pairs + p, 1), :] = h32[f * rows:f * rows + 1]
            rowf[1, pl.ds(f * pairs + p, 1), :] = h32[(f + 1) * rows - 1:(f + 1) * rows]
        for s in range(2):
            @pl.when(has_c[s] & (k == s))
            def _():
                c_copy(s).start()
        return carry

    lax.fori_loop(0, pairs, attend, 0)

    def r_copy(s):
        return pltpu.make_async_remote_copy(
            src_ref=rows_out.at[s], dst_ref=rows_in.at[1 - s],
            send_sem=r_send.at[s], recv_sem=r_recv.at[1 - s],
            device_id=(me_t, me_r + step[s], me_c), device_id_type=MESH,
        )

    def d_copy(i):
        return pltpu.make_async_remote_copy(
            src_ref=rows_out.at[i // 2], dst_ref=corn_in.at[3 - i],
            send_sem=d_send.at[i], recv_sem=d_recv.at[3 - i],
            device_id=diag[i][1], device_id_type=MESH,
        )

    rows_out[...] = rowf[...].astype(BF16)
    for s in range(2):
        @pl.when(has_r[s])
        def _():
            r_copy(s).start()
    for i in range(4):
        @pl.when(diag[i][0])
        def _():
            d_copy(i).start()
    for s in range(2):
        @pl.when(has_c[s])
        def _():
            c_copy(1 - s).wait_recv()

    row_at = lax.broadcasted_iota(jnp.int32, (rows, 1), 0)

    def convolve(p, carry):
        for f in range(2):
            at = pl.ds(f * rows, rows)
            h = hid[p, at].astype(F32)
            sw = swp[p + 1, at].astype(F32)
            mid_b = jnp.where(lane < 64, swp[p, at, 256:384].astype(F32), sw[:, 256:384])
            left = jnp.concatenate([swp[p, at, 0:256].astype(F32), mid_b, sw[:, 384:640]], 1)
            mid_a = jnp.where(lane < 64, sw[:, 256:384], swp[p + 2, at, 256:384].astype(F32))
            right = jnp.concatenate([sw[:, 0:256], mid_a, swp[p + 2, at, 384:640].astype(F32)], 1)
            acc = []
            for a in range(3):
                acc.append(
                    left * taps[3 * a:3 * a + 1]
                    + h * taps[3 * a + 1:3 * a + 2]
                    + right * taps[3 * a + 2:3 * a + 3]
                )
            down = jnp.where(row_at == 0, 0.0, pltpu.roll(acc[0], 1, 0))
            up = jnp.where(row_at == rows - 1, 0.0, pltpu.roll(acc[2], rows - 1, 0))
            acc_s[p, f] = (h + acc[1]) + (down + up)
        return carry

    lax.fori_loop(0, pairs, convolve, 0)

    for s in range(2):
        @pl.when(has_r[s])
        def _():
            r_copy(1 - s).wait_recv()
    for i in range(4):
        @pl.when(diag[i][0])
        def _():
            d_copy(3 - i).wait_recv()

    n_rows = rows_in.shape[1]
    pair_at = lax.broadcasted_iota(jnp.int32, (n_rows, 1), 0) % pairs
    first_half = lax.broadcasted_iota(jnp.int32, (1, wide), 1) < chans
    for s in range(2):
        line = rows_in[s].astype(F32)
        turned = pltpu.roll(line, chans, 1)
        left_c = pltpu.roll(corn_in[2 * s].astype(F32), chans, 1)
        right_c = pltpu.roll(corn_in[2 * s + 1].astype(F32), chans, 1)
        before = jnp.where(
            pair_at == 0, pltpu.roll(left_c, n_rows - (pairs - 1), 0), pltpu.roll(turned, 1, 0)
        )
        after = jnp.where(
            pair_at == pairs - 1,
            pltpu.roll(right_c, pairs - 1, 0),
            pltpu.roll(turned, n_rows - 1, 0),
        )
        tap = 6 * s
        edge[s] = (
            jnp.where(first_half, before, turned) * taps[tap:tap + 1]
            + line * taps[tap + 1:tap + 2]
            + jnp.where(first_half, turned, after) * taps[tap + 2:tap + 3]
        )

    def finish(p, carry):
        for f in range(2):
            above = edge[0, pl.ds(f * pairs + p, 1), :]
            below = edge[1, pl.ds(f * pairs + p, 1), :]
            head = acc_s[p, f, 0:8] + jnp.where(row_at[0:8] == 0, above, 0.0)
            foot = acc_s[p, f, rows - 8:] + jnp.where(row_at[rows - 8:] == rows - 1, below, 0.0)
            res = jnp.concatenate([head, acc_s[p, f, 8:rows - 8], foot], 0)
            out_ref[f, :, pl.ds(pl.multiple_of(p * wide, 128), wide)] = res.astype(BF16)
        return carry

    lax.fori_loop(0, pairs, finish, 0)

    for s in range(2):
        @pl.when(has_t[s])
        def _():
            def done(p, carry):
                t_copy(s, p).wait_send()
                return carry
            lax.fori_loop(0, pairs, done, 0)
        @pl.when(has_c[s])
        def _():
            c_copy(s).wait_send()
        @pl.when(has_r[s])
        def _():
            r_copy(s).wait_send()
    for i in range(4):
        @pl.when(diag[i][0])
        def _():
            d_copy(i).wait_send()


def body(sizes, latents, w_qkv, w_out, conv_weight):
    frames, rows, merged = latents.shape
    chans = w_out.shape[0]
    wide = 2 * chans
    pairs = merged // wide
    fr = frames * rows
    lines = -(-frames * pairs // 16) * 16
    vmem = pltpu.VMEM
    dma = pltpu.SemaphoreType.DMA
    scratch = [
        vmem(latents.shape, BF16), vmem(w_qkv.shape, BF16),
        vmem(w_out.shape, BF16), vmem(conv_weight.shape, F32),
        vmem((pairs, frames, rows, wide), F32),
        vmem((pairs, 2, frames, rows, wide), BF16),
        vmem((pairs, fr, wide), BF16),
        vmem((pairs, 3, fr, wide), BF16),
        vmem((pairs, 3, fr, wide), BF16),
        vmem((pairs, fr, wide), BF16),
        vmem((pairs + 2, fr, wide), BF16),
        vmem((2, lines, wide), F32),
        vmem((2, lines, wide), BF16),
        vmem((2, lines, wide), BF16),
        vmem((4, lines, wide), BF16),
        vmem((2, lines, wide), F32),
        vmem((384, 256), BF16), vmem((wide, 128), BF16), vmem((384, 256), BF16),
        vmem((384, 512), BF16), vmem((wide, 256), BF16), vmem((384, 512), BF16),
        vmem((384, 256), BF16), vmem((wide, 128), BF16), vmem((384, 256), BF16),
        vmem((9, wide), F32),
        vmem((wide, 256), BF16),
        vmem((256, 256), BF16),
        dma((2, pairs)), dma((2, pairs)),
        dma((2,)), dma((2,)), dma((2,)), dma((2,)), dma((4,)), dma((4,)), dma((4,)),
    ]
    cells = frames * rows * merged // chans
    return pl.pallas_call(
        functools.partial(kernel, sizes),
        out_shape=jax.ShapeDtypeStruct(latents.shape, BF16),
        in_specs=[pl.BlockSpec(memory_space=pl.ANY)] * 4,
        out_specs=pl.BlockSpec(memory_space=vmem),
        scratch_shapes=scratch,
        compiler_params=pltpu.CompilerParams(
            collective_id=0, has_side_effects=True, vmem_limit_bytes=53 * 2**20
        ),
        cost_estimate=pl.CostEstimate(
            flops=2 * cells * chans * chans * 8, bytes_accessed=4 * cells * chans,
            transcendentals=cells * 25,
        ),
    )(latents, w_qkv, w_out, conv_weight)


def solution(mesh):
    sizes = tuple(mesh.shape[name] for name in ("tm", "row", "col"))
    placed = (P("tm", "row", "col"), P(), P(), P())
    return jax.shard_map(
        functools.partial(body, sizes), mesh=mesh, in_specs=placed,
        out_specs=P("tm", "row", "col"), check_vma=False,
    )
```
